1024 devices in a mesh: dp: 16 (over x, y_lo), expert: 64 (over z, y_hi, core).
Axes of the slice: x: 8, y: 8 (y_hi: 4, y_lo: 2; y = y_hi * 2 + y_lo), z: 8, core: 2. Of those that a mesh axis runs over, the one named last changes fastest.
Arguments:
- tokens: bfloat16 [2, 4096, 7168], P(None, 'expert', 'dp'), may hold values from -6 to 6
- out_grad: bfloat16 [2, 4096, 7168], P(None, 'expert', 'dp'), may hold values from -6 to 6
- expert_ids: int32 [2, 4096, 1], P(None, 'expert'), may hold values from 0 to 15; in each aligned block of 64 rows (0 to 63, 64 to 127, ..., all dimensions but the last counted through in order) at most 8 rows name the same one
- gate_weights: float32 [2, 4096, 1], P(None, 'expert'), may hold values from 0.1 to 1
- w_up: bfloat16 [7168, 32768], P('dp', 'expert'), may hold values from -0.0625 to 0.0625
- w_down: bfloat16 [32768, 7168], P('expert', 'dp'), may hold values from -0.125 to 0.125
Outputs:
- mixed: bfloat16 [2, 4096, 7168], P(None, 'expert', 'dp')
- token_grad: bfloat16 [2, 4096, 7168], P(None, 'expert', 'dp')
- grad_up: bfloat16 [7168, 32768], P('dp', 'expert')
- grad_down: bfloat16 [32768, 7168], P('expert', 'dp')
The draws below stay inside these ranges and needn't reach their ends.
Inputs may be any that keep to these rules, and one draw needn't show every extreme that they name: `expert_ids`: within each micro-batch, the 64 tokens of one index of the expert axis (aligned blocks of 64 rows) name no expert more than 8 times; some expert is named exactly 8 times in some block.
All inputs are finite; a program needn't handle non-finite values.
Results may differ from the reference program's by a relative error of at most 0.03.
Values may be sent and summed in bfloat16 or wider, within the bound.
No kernel may reach another device: no remote copies, remote signals or barrier semaphores. Data moves between devices by JAX's collectives and lax.ppermute only.
A program may use at most 64 MiB of HBM per device.

```python
import math
import jax
import jax.numpy as jnp
import numpy as np
from jax import lax

D = 7168
FF = 2048
COLS = 4
MICRO = 2
TOK_DEV = 64
EXPERTS = 16
TOKENS = 4096
CAP = 8
N_DP = 16
N_EXPERT = 64


def level_of(key, dims, split, least, largest):
    factor_of, own = 1.0, jax.random.fold_in(key, 6)
    for axis_at, blocks in split:
        heights = jnp.exp(jax.random.uniform(jax.random.fold_in(own, axis_at), (blocks,), jnp.float32, least / len(split), largest / len(split)))
        factor_of = factor_of * jnp.repeat(heights, dims[axis_at] // blocks).reshape([-1 if axis == axis_at else 1 for axis in range(len(dims))])
    return factor_of


def shared_out(stream_key, own, number, rows, amount, top, limit, slope):
    ranking = jax.random.permutation(stream_key, amount)
    crowded, ordinary = load_shares(amount, rows * top, limit, slope, True), load_shares(amount, rows * top, limit, slope, False)
    places = jnp.arange(amount)

    def named(tallies, rotation):
        used = int((tallies > 0).sum())
        fixed = max(1, used // 4)
        moved = fixed + (places - fixed + rotation * (used - fixed)) % max(1, amount - fixed)
        return jnp.zeros((amount,), jnp.int32).at[ranking[jnp.where(places < fixed, places, moved)]].set(jnp.asarray(tallies, jnp.int32))

    tallies = jnp.where(number % 4 == 0, named(crowded, number // 4), named(ordinary, number - number // 4 - 1))
    mixed = jax.random.permutation(jax.random.fold_in(own, 3), amount)
    giver, taker = mixed[0:amount // 2 * 2:2], mixed[1:amount // 2 * 2:2]
    room = jnp.minimum(tallies[giver] - 1, limit - tallies[taker]) // 2
    room = jnp.where((giver == ranking[0]) | (taker == ranking[0]) | (tallies[taker] == 0), 0, jnp.maximum(room, 0))
    moved = jax.random.randint(jax.random.fold_in(own, 4), (amount // 2,), 0, 1 << 20) % (room + 1)
    tallies = tallies.at[giver].add(-moved).at[taker].add(moved)
    labels = jnp.searchsorted(jnp.cumsum(tallies), jnp.arange(rows * top), side="right").astype(jnp.int32)
    table = labels.reshape(top, rows).T
    table = table[jax.random.permutation(jax.random.fold_in(own, 1), rows)]
    rotation = jax.random.randint(jax.random.fold_in(own, 2), (rows, 1), 0, top)
    return jnp.take_along_axis(table, (jnp.arange(top)[None, :] + rotation) % top, axis=1)


def load_shares(count, total, reach, skew, full):
    portions = [(1 << 20) // math.isqrt(standing ** skew) + 1 for standing in range(1, count + 1)]
    largest = reach if full else min(reach, max(-(-total // count), total * portions[0] // sum(portions)))
    least = 1 if total - largest >= count - 1 else 0
    given, surplus = [largest] + [least] * (count - 1), total - largest - least * (count - 1)
    while surplus > 0:
        candidates = [i for i in range(1, count) if given[i] < largest] or [i for i in range(1, count) if given[i] < reach]
        pool, left = sum([portions[i] for i in candidates]), surplus
        for i in candidates:
            extra = min(reach - given[i], max(1, left * portions[i] // pool), surplus)
            given[i] = given[i] + extra
            surplus = surplus - extra
    return np.array(given)


def gaussian(own_key, dims, spread, limit, cuts=(), held_as=jnp.bfloat16):
    result = spread * jax.random.normal(own_key, dims, jnp.float32)
    if cuts:
        result = result * level_of(own_key, dims, cuts, -0.22, 0.18)
    return jnp.clip(result, -limit, limit).astype(held_as)


def setup_inputs(seed: int = 0) -> dict:
    streams_of = jax.random.split(jax.random.key(seed), 7)
    tokens = gaussian(streams_of[0], (MICRO, TOKENS, D), 1.0, 6.0, ((1, 64), (2, 16)))
    out_grad = gaussian(streams_of[1], (MICRO, TOKENS, D), 1.0, 6.0, ((1, 64), (2, 16)))
    expert_ids_keys = jax.random.split(jax.random.fold_in(streams_of[2], 1), MICRO * TOKENS // TOK_DEV)
    expert_ids_turns = jax.random.permutation(jax.random.fold_in(streams_of[2], 3), MICRO * TOKENS // TOK_DEV)
    expert_ids = jax.vmap(lambda own, number: shared_out(jax.random.fold_in(streams_of[2], 2), own, number, TOK_DEV, EXPERTS, 1, CAP, 2))(expert_ids_keys, expert_ids_turns).reshape((MICRO, TOKENS, 1))
    gate_weights = jnp.clip(0.1 + 0.9 * jax.random.uniform(streams_of[3], (MICRO, TOKENS, 1), jnp.float32) ** level_of(streams_of[3], (MICRO, TOKENS, 1), ((1, 64),), -0.2, 0.2), 0.1, 1.0)
    w_up = gaussian(streams_of[4], (D, EXPERTS * FF), D ** -0.5, 0.0625, ((0, 16), (1, 64)))
    w_down = gaussian(streams_of[5], (EXPERTS * FF, D), FF ** -0.5, 0.125, ((0, 64), (1, 16)))
    return {"tokens": tokens, "out_grad": out_grad, "expert_ids": expert_ids, "gate_weights": gate_weights, "w_up": w_up, "w_down": w_down}


def silu_grad(preact):
    logistic = jax.nn.sigmoid(preact)
    return logistic * (1.0 + preact * (1.0 - logistic))

def block_sum(left, right, blocks):
    row_count = left.shape[0]
    inner_size = left.shape[1]
    outer_size = right.shape[1]
    pieces = jnp.einsum('rnk,nkm->nrm', left.astype(jnp.float32).reshape(row_count, blocks, inner_size // blocks), right.astype(jnp.float32).reshape(blocks, inner_size // blocks, outer_size), precision=lax.Precision.HIGHEST)
    rounded = lax.optimization_barrier(pieces.astype(jnp.bfloat16))
    return lax.optimization_barrier(jnp.sum(rounded.astype(jnp.float32), axis=0))

def slot_rows(routing):
    choose = (routing[:, None] == jnp.arange(EXPERTS, dtype=jnp.int32)[None, :]).astype(jnp.int32)
    running = jnp.cumsum(choose.reshape(N_EXPERT, TOK_DEV, EXPERTS), axis=1).reshape(TOKENS, EXPERTS)
    position = lax.optimization_barrier(jnp.sum((running - 1) * choose, axis=1))
    source = jnp.arange(TOKENS, dtype=jnp.int32) // TOK_DEV
    return (routing * (N_EXPERT * CAP) + source * CAP + position).astype(jnp.int32)

def expert_pass(packed):
    inputs, scaled, up_weight, down_weight = packed
    outputs = []
    grads_back = []
    grad_in = jnp.zeros((D, FF), jnp.float32)
    grad_out = jnp.zeros((FF, D), jnp.float32)
    for micro_index in range(MICRO):
        rows_in = inputs[micro_index]
        rows_grad = scaled[micro_index]
        preact = block_sum(rows_in, up_weight, N_DP)
        hidden = jax.nn.silu(preact).astype(jnp.bfloat16)
        outputs.append(block_sum(hidden, down_weight, COLS))
        back_term = block_sum(rows_grad, down_weight.T, N_DP)
        preact_grad = (back_term * silu_grad(preact)).astype(jnp.bfloat16)
        grads_back.append(block_sum(preact_grad, up_weight.T, COLS))
        grad_in = grad_in + jnp.dot(rows_in.T, preact_grad, preferred_element_type=jnp.float32)
        grad_out = grad_out + jnp.dot(hidden.T, rows_grad, preferred_element_type=jnp.float32)
    return (jnp.stack(outputs), jnp.stack(grads_back), grad_in, grad_out)

def reference(tokens, out_grad, expert_ids, gate_weights, w_up, w_down):
    per_expert = N_EXPERT * CAP
    targets = []
    inputs = []
    scaled_all = []
    for micro_index in range(MICRO):
        target = slot_rows(expert_ids[micro_index, :, 0])
        scaled = (gate_weights[micro_index] * out_grad[micro_index].astype(jnp.float32)).astype(jnp.bfloat16)
        inputs.append(jnp.zeros((EXPERTS * per_expert, D), jnp.bfloat16).at[target].set(tokens[micro_index]))
        scaled_all.append(jnp.zeros((EXPERTS * per_expert, D), jnp.bfloat16).at[target].set(scaled))
        targets.append(target)
    stacked_in = jnp.stack(inputs).reshape(MICRO, EXPERTS, per_expert, D).transpose(1, 0, 2, 3)
    stacked_grad = jnp.stack(scaled_all).reshape(MICRO, EXPERTS, per_expert, D).transpose(1, 0, 2, 3)
    up_blocks = w_up.reshape(D, EXPERTS, FF).transpose(1, 0, 2)
    down_blocks = w_down.reshape(EXPERTS, FF, D)
    mixed_rows, back_rows, grad_in, grad_out = lax.map(expert_pass, (stacked_in, stacked_grad, up_blocks, down_blocks))
    mixed_list = []
    token_list = []
    for micro_index in range(MICRO):
        flat_mixed = mixed_rows[:, micro_index].reshape(EXPERTS * per_expert, D)
        flat_back = back_rows[:, micro_index].reshape(EXPERTS * per_expert, D)
        mixed_list.append((gate_weights[micro_index] * flat_mixed[targets[micro_index]]).astype(jnp.bfloat16))
        token_list.append(flat_back[targets[micro_index]].astype(jnp.bfloat16))
    grad_up = grad_in.transpose(1, 0, 2).reshape(D, EXPERTS * FF).astype(jnp.bfloat16)
    grad_down = grad_out.reshape(EXPERTS * FF, D).astype(jnp.bfloat16)
    return (jnp.stack(mixed_list), jnp.stack(token_list), grad_up, grad_down)
```

```python
import jax
import jax.numpy as jnp
from jax import lax
from jax.sharding import PartitionSpec as P

FF = 2048
GROUPS = ((0, 1),)


def silu_grad(preact):
    logistic = jax.nn.sigmoid(preact)
    return logistic * (1.0 + preact * (1.0 - logistic))


def on_device(tokens, out_grad, expert_ids, gate_weights, w_up, w_down):
    micro_count, token_count, features = tokens.shape
    hidden_cols = w_up.shape[1]
    columns = lax.axis_size("expert")
    dp = lax.axis_size("dp")
    groups_per = FF // hidden_cols
    chips_per = groups_per // 2
    experts = columns // groups_per
    capacity = 2 * token_count // experts
    slot_count = experts * capacity
    bf16 = jnp.bfloat16
    f32 = jnp.float32
    contract_last = (((1,), (1,)), ((), ()))
    contract_first = (((0,), (0,)), ((), ()))
    pairs = [[2 * i, 2 * i + 1] for i in range(columns // 2)]
    swap = [(i, i ^ 1) for i in range(columns)]
    first_core = lax.rem(lax.axis_index("expert"), 2) == 0

    routing = expert_ids[:, :, 0]
    earlier = jnp.tril(jnp.ones((token_count, token_count), jnp.bool_), -1)
    same = (routing[:, :, None] == routing[:, None, :]) & earlier[None]
    slots = routing * capacity + jnp.sum(same.astype(jnp.int32), axis=2)
    slot_range = jnp.arange(slot_count, dtype=jnp.int32)
    table = (slots[:, None, :] == slot_range[None, :, None]).astype(bf16)
    table_back = (slots[:, :, None] == slot_range[None, None, :]).astype(bf16)
    scaled = (gate_weights * out_grad.astype(f32)).astype(bf16)

    def dispatch(micros):
        count = len(micros)
        both = jnp.stack([tokens[micros[0] : micros[-1] + 1], scaled[micros[0] : micros[-1] + 1]])
        packed = jnp.einsum(
            "mst,amtf->amsf", table[micros[0] : micros[-1] + 1], both, preferred_element_type=f32
        ).astype(bf16)
        packed = packed.reshape(2, count, experts, capacity, features).transpose(2, 0, 1, 3, 4)
        packed = packed.reshape(experts, 1, 2, count * capacity, features)
        packed = jnp.broadcast_to(packed, (experts, chips_per, 2, count * capacity, features))
        packed = packed.reshape(columns, count * capacity, features)
        arrived = lax.all_to_all(packed, "expert", 0, 0, tiled=True)
        arrived = arrived.reshape(2, 1, columns * count * capacity // 2, features)
        halves = [
            lax.all_gather(half, "expert", axis=0, axis_index_groups=pairs, tiled=True)
            for half in (arrived[0], arrived[1])
        ]
        return [half[0] for half in halves], [half[1] for half in halves]

    def reduce_middle(rows_in, rows_grad):
        halves = []
        for one_in, one_grad in zip(rows_in, rows_grad):
            pre = jnp.dot(one_in, w_up, preferred_element_type=f32)
            back = lax.dot_general(one_grad, w_down, contract_last, preferred_element_type=f32)
            halves.append(jnp.concatenate([pre.astype(bf16), back.astype(bf16)], axis=1))
        parts = jnp.concatenate(halves, axis=0).reshape(dp, -1, 2 * hidden_cols)
        got = lax.all_to_all(parts, "dp", 0, 0, tiled=True)
        return jnp.sum(got.astype(f32), axis=0)

    def gather_middle(total):
        pre, back = total[:, :hidden_cols], total[:, hidden_cols:]
        share = jnp.concatenate(
            [jax.nn.silu(pre).astype(bf16), (back * silu_grad(pre)).astype(bf16)], axis=1
        )
        share = jnp.broadcast_to(share[None], (dp,) + share.shape)
        full = lax.all_to_all(share, "dp", 0, 0, tiled=True).reshape(-1, 2 * hidden_cols)
        return full[:, :hidden_cols], full[:, hidden_cols:]

    def combine(micros, hidden, preact_grad):
        count = len(micros)
        mixed_part = jnp.dot(hidden, w_down, preferred_element_type=f32).astype(bf16)
        token_part = lax.dot_general(
            preact_grad, w_up, contract_last, preferred_element_type=f32
        ).astype(bf16)
        keep = jnp.where(first_core, mixed_part, token_part)
        give = jnp.where(first_core, token_part, mixed_part)
        came = lax.ppermute(give, "expert", swap)
        total = (keep.astype(f32) + came.astype(f32)).astype(bf16)
        back = lax.all_to_all(
            total.reshape(columns, count * capacity, features), "expert", 0, 0, tiled=True
        )
        back = back.reshape(experts, chips_per, 2, count, capacity, features)
        back = back.transpose(2, 3, 1, 0, 4, 5).reshape(2, count, chips_per * slot_count, features)
        spread = jnp.concatenate([table_back[micros[0] : micros[-1] + 1]] * chips_per, axis=2)
        return jnp.einsum("mts,amsf->amtf", spread, back, preferred_element_type=f32)

    rows = [dispatch(micros) for micros in GROUPS]
    totals = [reduce_middle(*r) for r in rows]
    middles = [gather_middle(t) for t in totals]
    outs = [combine(micros, *m) for micros, m in zip(GROUPS, middles)]
    grad_in = 0.0
    grad_out = 0.0
    for (rows_in, rows_grad), (hidden, preact_grad) in zip(rows, middles):
        start = 0
        for one_in, one_grad in zip(rows_in, rows_grad):
            stop = start + one_in.shape[0]
            grad_in = grad_in + lax.dot_general(
                one_in, preact_grad[start:stop], contract_first, preferred_element_type=f32
            )
            grad_out = grad_out + lax.dot_general(
                hidden[start:stop], one_grad, contract_first, preferred_element_type=f32
            )
            start = stop
    both = jnp.concatenate(outs, axis=1)
    return (
        (gate_weights * both[0]).astype(bf16),
        both[1].astype(bf16),
        grad_in.astype(bf16),
        grad_out.astype(bf16),
    )


def solution(mesh):
    in_specs = (
        P(None, "expert", "dp"),
        P(None, "expert", "dp"),
        P(None, "expert", None),
        P(None, "expert", None),
        P("dp", "expert"),
        P("expert", "dp"),
    )
    out_specs = (
        P(None, "expert", "dp"),
        P(None, "expert", "dp"),
        P("dp", "expert"),
        P("expert", "dp"),
    )
    return jax.shard_map(
        on_device, mesh=mesh, in_specs=in_specs, out_specs=out_specs, check_vma=False
    )
```

```python
import jax
import jax.numpy as jnp
from jax import lax
from jax.sharding import PartitionSpec as P

FF = 2048


def silu_grad(preact):
    logistic = jax.nn.sigmoid(preact)
    return logistic * (1.0 + preact * (1.0 - logistic))


def on_device(tokens, out_grad, expert_ids, gate_weights, w_up, w_down):
    micro_count, token_count, features = tokens.shape
    hidden_cols = w_up.shape[1]
    columns = lax.axis_size("expert")
    dp = lax.axis_size("dp")
    lines = dp // 2
    groups_per = FF // hidden_cols
    chips_per = groups_per // 2
    experts = columns // groups_per
    capacity = 2 * token_count // experts
    slot_count = experts * capacity
    wide = 2 * features
    bf16 = jnp.bfloat16
    f32 = jnp.float32
    contract_last = (((1,), (1,)), ((), ()))
    contract_first = (((0,), (0,)), ((), ()))
    cores = [[2 * i, 2 * i + 1] for i in range(columns // 2)]
    swap_core = [(i, i ^ 1) for i in range(columns)]
    swap_side = [(i, i ^ 1) for i in range(dp)]
    along_x = [[2 * i + side for i in range(lines)] for side in range(2)]
    first_core = lax.rem(lax.axis_index("expert"), 2) == 0
    mine = lax.rem(lax.axis_index("dp"), 2)

    def pick(array, index):
        return lax.dynamic_index_in_dim(array, index, 0, keepdims=False)

    both = jnp.stack(
        [tokens, (gate_weights * out_grad.astype(f32)).astype(bf16)], axis=1
    )
    came_rows = lax.ppermute(pick(both, 1 - mine), "dp", swap_side)
    came_up = lax.ppermute(w_up, "dp", swap_side)
    came_down = lax.ppermute(w_down.T, "dp", swap_side)
    up = jnp.concatenate([w_up, came_up], axis=0)
    down_t = jnp.concatenate([w_down.T, came_down], axis=0)

    routing = pick(expert_ids, mine)[:, 0]
    gate = pick(gate_weights, mine)
    earlier = jnp.tril(jnp.ones((token_count, token_count), jnp.bool_), -1)
    same = (routing[:, None] == routing[None, :]) & earlier
    slots = routing * capacity + jnp.sum(same.astype(jnp.int32), axis=1)
    slot_range = jnp.arange(slot_count, dtype=jnp.int32)
    table = (slots[None, :] == slot_range[:, None]).astype(bf16)
    table_back = (slots[:, None] == slot_range[None, :]).astype(bf16)

    sent = jnp.concatenate([pick(both, mine), came_rows], axis=2)
    packed = jnp.einsum("st,atf->asf", table, sent, preferred_element_type=f32).astype(bf16)
    packed = packed.reshape(2, experts, capacity, wide).transpose(1, 0, 2, 3)
    packed = jnp.broadcast_to(packed[:, None], (experts, chips_per, 2, capacity, wide))
    packed = packed.reshape(columns, capacity, wide)
    arrived = lax.all_to_all(packed, "expert", 0, 0, tiled=True)
    arrived = arrived.reshape(2, 1, columns * capacity // 2, wide)
    halves = [
        lax.all_gather(half, "expert", axis=0, axis_index_groups=cores, tiled=True)
        for half in (arrived[0], arrived[1])
    ]

    parts = []
    for half in halves:
        pre = jnp.dot(half[0], up, preferred_element_type=f32)
        back = jnp.dot(half[1], down_t, preferred_element_type=f32)
        parts.append(jnp.concatenate([pre.astype(bf16), back.astype(bf16)], axis=1))
    parts = jnp.concatenate(parts, axis=0).reshape(lines, -1, 2 * hidden_cols)
    got = lax.all_to_all(parts, "dp", 0, 0, axis_index_groups=along_x, tiled=True)
    total = jnp.sum(got.astype(f32), axis=0)
    pre, back = total[:, :hidden_cols], total[:, hidden_cols:]
    share = jnp.concatenate(
        [jax.nn.silu(pre).astype(bf16), (back * silu_grad(pre)).astype(bf16)], axis=1
    )
    share = jnp.broadcast_to(share[None], (lines,) + share.shape)
    full = lax.all_to_all(share, "dp", 0, 0, axis_index_groups=along_x, tiled=True)
    full = full.reshape(-1, 2 * hidden_cols)
    hidden, preact_grad = full[:, :hidden_cols], full[:, hidden_cols:]

    mixed_part = lax.dot_general(
        hidden, down_t, contract_last, preferred_element_type=f32
    ).astype(bf16)
    token_part = lax.dot_general(
        preact_grad, up, contract_last, preferred_element_type=f32
    ).astype(bf16)
    keep = jnp.where(first_core, mixed_part, token_part)
    give = jnp.where(first_core, token_part, mixed_part)
    came = lax.ppermute(give, "expert", swap_core)
    chip_sum = (keep.astype(f32) + came.astype(f32)).astype(bf16)
    home = lax.all_to_all(
        chip_sum.reshape(columns, capacity, wide), "expert", 0, 0, tiled=True
    )
    home = home.reshape(experts, chips_per, 2, capacity, wide).transpose(2, 1, 0, 3, 4)
    home = home.reshape(2, chips_per * slot_count, wide)
    spread = jnp.concatenate([table_back] * chips_per, axis=1)
    summed = jnp.einsum("ts,asf->atf", spread, home, preferred_element_type=f32)
    done = jnp.stack([gate * summed[0], summed[1]]).astype(bf16)
    came_done = lax.ppermute(done[:, :, features:], "dp", swap_side)
    own_done = done[:, :, :features]
    first = jnp.where(mine == 0, own_done, came_done)
    second = jnp.where(mine == 0, came_done, own_done)

    grad_up = 0.0
    grad_down_t = 0.0
    rows = columns * capacity // 2
    for number, half in enumerate(halves):
        at = slice(number * rows, (number + 1) * rows)
        grad_up = grad_up + lax.dot_general(
            half[0], preact_grad[at], contract_first, preferred_element_type=f32
        )
        grad_down_t = grad_down_t + lax.dot_general(
            half[1], hidden[at], contract_first, preferred_element_type=f32
        )
    came_grad_up = lax.ppermute(grad_up[features:].astype(bf16), "dp", swap_side)
    came_grad_down = lax.ppermute(grad_down_t[features:].astype(bf16), "dp", swap_side)
    grad_up = grad_up[:features] + came_grad_up.astype(f32)
    grad_down_t = grad_down_t[:features] + came_grad_down.astype(f32)
    return (
        jnp.stack([first[0], second[0]]),
        jnp.stack([first[1], second[1]]),
        grad_up.astype(bf16),
        grad_down_t.astype(bf16).T,
    )


def solution(mesh):
    in_specs = (
        P(None, "expert", "dp"),
        P(None, "expert", "dp"),
        P(None, "expert", None),
        P(None, "expert", None),
        P("dp", "expert"),
        P("expert", "dp"),
    )
    out_specs = (
        P(None, "expert", "dp"),
        P(None, "expert", "dp"),
        P("dp", "expert"),
        P("expert", "dp"),
    )
    return jax.shard_map(
        on_device, mesh=mesh, in_specs=in_specs, out_specs=out_specs, check_vma=False
    )
```

```python
import jax
import jax.numpy as jnp
from jax import lax
from jax.sharding import PartitionSpec as P

FF = 2048


def silu_grad(preact):
    logistic = jax.nn.sigmoid(preact)
    return logistic * (1.0 + preact * (1.0 - logistic))


def on_device(tokens, out_grad, expert_ids, gate_weights, w_up, w_down):
    micro_count, token_count, features = tokens.shape
    hidden_cols = w_up.shape[1]
    columns = lax.axis_size("expert")
    dp = lax.axis_size("dp")
    lines = dp // 2
    groups_per = FF // hidden_cols
    chips_per = groups_per // 2
    experts = columns // groups_per
    capacity = 2 * token_count // experts
    slot_count = experts * capacity
    wide = 2 * features
    bf16 = jnp.bfloat16
    f32 = jnp.float32
    contract_last = (((1,), (1,)), ((), ()))
    contract_first = (((0,), (0,)), ((), ()))
    cores = [[2 * i, 2 * i + 1] for i in range(columns // 2)]
    swap_core = [(i, i ^ 1) for i in range(columns)]
    swap_side = [(i, i ^ 2) for i in range(dp)]
    peers = [[i for i in range(dp) if i // 2 % 2 == side] for side in range(2)]
    first_core = lax.rem(lax.axis_index("expert"), 2) == 0
    mine = lax.rem(lax.axis_index("dp") // 2, 2)

    def pick(array, index):
        return lax.dynamic_index_in_dim(array, index, 0, keepdims=False)

    both = jnp.stack(
        [tokens, (gate_weights * out_grad.astype(f32)).astype(bf16)], axis=1
    )
    came_rows = lax.ppermute(pick(both, 1 - mine), "dp", swap_side)
    came_up = lax.ppermute(w_up, "dp", swap_side)
    came_down = lax.ppermute(w_down.T, "dp", swap_side)
    up = jnp.concatenate([w_up, came_up], axis=0)
    down_t = jnp.concatenate([w_down.T, came_down], axis=0)

    routing = pick(expert_ids, mine)[:, 0]
    gate = pick(gate_weights, mine)
    earlier = jnp.tril(jnp.ones((token_count, token_count), jnp.bool_), -1)
    same = (routing[:, None] == routing[None, :]) & earlier
    slots = routing * capacity + jnp.sum(same.astype(jnp.int32), axis=1)
    slot_range = jnp.arange(slot_count, dtype=jnp.int32)
    table = (slots[None, :] == slot_range[:, None]).astype(bf16)
    table_back = (slots[:, None] == slot_range[None, :]).astype(bf16)

    sent = jnp.concatenate([pick(both, mine), came_rows], axis=2)
    packed = jnp.einsum("st,atf->asf", table, sent, preferred_element_type=f32).astype(bf16)
    packed = packed.reshape(2, experts, capacity, wide).transpose(1, 0, 2, 3)
    packed = jnp.broadcast_to(packed[:, None], (experts, chips_per, 2, capacity, wide))
    packed = packed.reshape(columns, capacity, wide)
    arrived = lax.all_to_all(packed, "expert", 0, 0, tiled=True)
    arrived = arrived.reshape(2, 1, columns * capacity // 2, wide)
    halves = [
        lax.all_gather(half, "expert", axis=0, axis_index_groups=cores, tiled=True)
        for half in (arrived[0], arrived[1])
    ]

    parts = []
    for half in halves:
        pre = jnp.dot(half[0], up, preferred_element_type=f32)
        back = jnp.dot(half[1], down_t, preferred_element_type=f32)
        parts.append(jnp.concatenate([pre.astype(bf16), back.astype(bf16)], axis=1))
    parts = jnp.concatenate(parts, axis=0).reshape(lines, -1, 2 * hidden_cols)
    got = lax.all_to_all(parts, "dp", 0, 0, axis_index_groups=peers, tiled=True)
    total = jnp.sum(got.astype(f32), axis=0)
    pre, back = total[:, :hidden_cols], total[:, hidden_cols:]
    share = jnp.concatenate(
        [jax.nn.silu(pre).astype(bf16), (back * silu_grad(pre)).astype(bf16)], axis=1
    )
    share = jnp.broadcast_to(share[None], (lines,) + share.shape)
    full = lax.all_to_all(share, "dp", 0, 0, axis_index_groups=peers, tiled=True)
    full = full.reshape(-1, 2 * hidden_cols)
    hidden, preact_grad = full[:, :hidden_cols], full[:, hidden_cols:]

    mixed_part = lax.dot_general(
        hidden, down_t, contract_last, preferred_element_type=f32
    ).astype(bf16)
    token_part = lax.dot_general(
        preact_grad, up, contract_last, preferred_element_type=f32
    ).astype(bf16)
    keep = jnp.where(first_core, mixed_part, token_part)
    give = jnp.where(first_core, token_part, mixed_part)
    came = lax.ppermute(give, "expert", swap_core)
    chip_sum = (keep.astype(f32) + came.astype(f32)).astype(bf16)
    home = lax.all_to_all(
        chip_sum.reshape(columns, capacity, wide), "expert", 0, 0, tiled=True
    )
    home = home.reshape(experts, chips_per, 2, capacity, wide).transpose(2, 1, 0, 3, 4)
    home = home.reshape(2, chips_per * slot_count, wide)
    spread = jnp.concatenate([table_back] * chips_per, axis=1)
    summed = jnp.einsum("ts,asf->atf", spread, home, preferred_element_type=f32)
    done = jnp.stack([gate * summed[0], summed[1]]).astype(bf16)
    came_done = lax.ppermute(done[:, :, features:], "dp", swap_side)
    own_done = done[:, :, :features]
    first = jnp.where(mine == 0, own_done, came_done)
    second = jnp.where(mine == 0, came_done, own_done)

    grad_up = 0.0
    grad_down_t = 0.0
    rows = columns * capacity // 2
    for number, half in enumerate(halves):
        at = slice(number * rows, (number + 1) * rows)
        grad_up = grad_up + lax.dot_general(
            half[0], preact_grad[at], contract_first, preferred_element_type=f32
        )
        grad_down_t = grad_down_t + lax.dot_general(
            half[1], hidden[at], contract_first, preferred_element_type=f32
        )
    came_grad_up = lax.ppermute(grad_up[features:].astype(bf16), "dp", swap_side)
    came_grad_down = lax.ppermute(grad_down_t[features:].astype(bf16), "dp", swap_side)
    grad_up = grad_up[:features] + came_grad_up.astype(f32)
    grad_down_t = grad_down_t[:features] + came_grad_down.astype(f32)
    return (
        jnp.stack([first[0], second[0]]),
        jnp.stack([first[1], second[1]]),
        grad_up.astype(bf16),
        grad_down_t.astype(bf16).T,
    )


def solution(mesh):
    in_specs = (
        P(None, "expert", "dp"),
        P(None, "expert", "dp"),
        P(None, "expert", None),
        P(None, "expert", None),
        P("dp", "expert"),
        P("expert", "dp"),
    )
    out_specs = (
        P(None, "expert", "dp"),
        P(None, "expert", "dp"),
        P("dp", "expert"),
        P("expert", "dp"),
    )
    return jax.shard_map(
        on_device, mesh=mesh, in_specs=in_specs, out_specs=out_specs, check_vma=False
    )
```

```python
import jax
import jax.numpy as jnp
from jax import lax
from jax.sharding import PartitionSpec as P

FF = 2048


def silu_grad(preact):
    logistic = jax.nn.sigmoid(preact)
    return logistic * (1.0 + preact * (1.0 - logistic))


def on_device(tokens, out_grad, expert_ids, gate_weights, w_up, w_down):
    micro_count, token_count, features = tokens.shape
    hidden_cols = w_up.shape[1]
    columns = lax.axis_size("expert")
    dp = lax.axis_size("dp")
    lines = dp // 2
    groups_per = FF // hidden_cols
    chips_per = groups_per // 2
    experts = columns // groups_per
    capacity = 2 * token_count // experts
    wide = 2 * features
    bf16 = jnp.bfloat16
    f32 = jnp.float32
    contract_last = (((1,), (1,)), ((), ()))
    contract_first = (((0,), (0,)), ((), ()))
    swap_core = [(i, i ^ 1) for i in range(columns)]
    swap_side = [(i, i ^ 2) for i in range(dp)]
    peers = [[i for i in range(dp) if i // 2 % 2 == side] for side in range(2)]
    first_core = (lax.axis_index("expert") & 1) == 0
    on_second = (lax.axis_index("dp") & 2) == 2

    def pick(array):
        return jnp.where(on_second, array[1], array[0])

    given = jnp.stack(
        [jnp.where(on_second, array[0], array[1]) for array in (tokens, out_grad)]
    )
    came_rows = lax.ppermute(given, "dp", swap_side)

    w_down_t = w_down.T
    in_own = jnp.where(first_core, w_up, w_down_t)
    out_own = jnp.where(first_core, w_down_t, w_up)
    in_own = jnp.concatenate([in_own, lax.ppermute(in_own, "dp", swap_side)], axis=0)
    out_own = jnp.concatenate([out_own, lax.ppermute(out_own, "dp", swap_side)], axis=0)
    in_other = lax.ppermute(out_own, "expert", swap_core)
    out_other = lax.ppermute(in_own, "expert", swap_core)
    in_both = lax.optimization_barrier(jnp.concatenate([in_own, in_other], axis=1))
    out_both = lax.optimization_barrier(jnp.concatenate([out_own, out_other], axis=1))

    routing = pick(expert_ids)[:, 0]
    gate = pick(gate_weights)
    ones = jnp.ones_like(gate)
    earlier = jnp.tril(jnp.ones((token_count, token_count), jnp.bool_), -1)
    same = (routing[:, None] == routing[None, :]) & earlier
    slots = routing * capacity + jnp.sum(same.astype(jnp.int32), axis=1)
    row = jnp.arange(columns * capacity, dtype=jnp.int32)
    device, place = row // capacity, row % capacity
    row_key = (device // groups_per * capacity + place) * 2 + device % 2
    column_key = jnp.concatenate([2 * slots, 2 * slots + 1])
    table = (row_key[:, None] == column_key[None, :]).astype(bf16)

    held = jnp.stack([pick(tokens), pick(out_grad)])
    sent = jnp.concatenate([held, came_rows], axis=2).astype(f32)
    sent = (jnp.stack([ones, gate]) * sent).astype(bf16).reshape(2 * token_count, wide)
    packed = jnp.dot(table, sent, preferred_element_type=f32).astype(bf16)
    packed = packed.reshape(columns, capacity, wide)
    rows = lax.all_to_all(packed, "expert", 0, 0, tiled=True)
    rows = rows.reshape(columns * capacity, wide)
    other_rows = lax.ppermute(rows, "expert", swap_core)

    parts = jnp.dot(rows, in_both, preferred_element_type=f32).astype(bf16)
    parts = parts.reshape(lines, -1, 2 * hidden_cols)
    got = lax.all_to_all(parts, "dp", 0, 0, axis_index_groups=peers, tiled=True)
    total = jnp.sum(got.astype(f32), axis=0)
    pre = lax.ppermute(total, "expert", swap_core)
    pre = jnp.concatenate([pre[:, hidden_cols:], pre[:, :hidden_cols]], axis=1)
    share = jnp.where(first_core, jax.nn.silu(total), total * silu_grad(pre)).astype(bf16)
    share = jnp.broadcast_to(share[None], (lines,) + share.shape)
    full = lax.all_to_all(share, "dp", 0, 0, axis_index_groups=peers, tiled=True)
    full = full.reshape(-1, 2 * hidden_cols)
    chip_sum = lax.dot_general(
        full, out_both, contract_last, preferred_element_type=f32
    ).astype(bf16)

    home = lax.all_to_all(
        chip_sum.reshape(columns, capacity, wide), "expert", 0, 0, tiled=True
    )
    summed = lax.dot_general(
        table, home.reshape(-1, wide), contract_first, preferred_element_type=f32
    )
    done = (jnp.stack([gate, ones]) * summed.reshape(2, token_count, wide)).astype(bf16)
    came_done = lax.ppermute(done[:, :, features:], "dp", swap_side)
    own_done = done[:, :, :features]
    is_mine = (jnp.arange(micro_count) == 1)[:, None, None] == on_second

    def grad_of(columns_of):
        whole = lax.dot_general(
            other_rows, columns_of, contract_first, preferred_element_type=f32
        )
        came = lax.ppermute(whole[features:].astype(bf16), "dp", swap_side)
        return (whole[:features] + came.astype(f32)).astype(bf16)

    grad_given = grad_of(full[:, hidden_cols:])
    grad_came = lax.ppermute(grad_given, "expert", swap_core)
    grad_own = grad_of(full[:, :hidden_cols])
    return (
        jnp.where(is_mine, own_done[0][None], came_done[0][None]),
        jnp.where(is_mine, own_done[1][None], came_done[1][None]),
        jnp.where(first_core, grad_came, grad_own),
        jnp.where(first_core, grad_own, grad_came).T,
    )


def solution(mesh):
    in_specs = (
        P(None, "expert", "dp"),
        P(None, "expert", "dp"),
        P(None, "expert", None),
        P(None, "expert", None),
        P("dp", "expert"),
        P("expert", "dp"),
    )
    out_specs = (
        P(None, "expert", "dp"),
        P(None, "expert", "dp"),
        P("dp", "expert"),
        P("expert", "dp"),
    )
    return jax.shard_map(
        on_device, mesh=mesh, in_specs=in_specs, out_specs=out_specs, check_vma=False
    )
```

```python
import jax
import jax.numpy as jnp
from jax import lax
from jax.sharding import PartitionSpec as P

FF = 2048


def silu_grad(preact):
    logistic = jax.nn.sigmoid(preact)
    return logistic * (1.0 + preact * (1.0 - logistic))


def on_device(tokens, out_grad, expert_ids, gate_weights, w_up, w_down):
    micro_count, token_count, features = tokens.shape
    hidden_cols = w_up.shape[1]
    columns = lax.axis_size("expert")
    dp = lax.axis_size("dp")
    lines = dp // 2
    groups_per = FF // hidden_cols
    chips_per = groups_per // 2
    experts = columns // groups_per
    capacity = 2 * token_count // experts
    wide = 2 * features
    bf16 = jnp.bfloat16
    f32 = jnp.float32
    contract_last = (((1,), (1,)), ((), ()))
    contract_first = (((0,), (0,)), ((), ()))
    swap_core = [(i, i ^ 1) for i in range(columns)]
    swap_side = [(i, i ^ 2) for i in range(dp)]
    peers = [[i for i in range(dp) if i // 2 % 2 == side] for side in range(2)]
    first_core = (lax.axis_index("expert") & 1) == 0
    on_second = (lax.axis_index("dp") & 2) == 2

    def pick(array):
        return jnp.where(on_second, array[1], array[0])

    given = jnp.stack(
        [jnp.where(on_second, array[0], array[1]) for array in (tokens, out_grad)]
    )
    came_rows = lax.ppermute(given, "dp", swap_side)

    w_down_t = w_down.T
    weights = jnp.concatenate(
        [jnp.where(first_core, w_up, w_down_t), jnp.where(first_core, w_down_t, w_up)], axis=1
    )
    weights = jnp.concatenate([weights, lax.ppermute(weights, "dp", swap_side)], axis=0)
    weights = lax.optimization_barrier(weights)
    first, second = weights[:, :hidden_cols], weights[:, hidden_cols:]

    routing = pick(expert_ids)[:, 0]
    gate = pick(gate_weights)
    ones = jnp.ones_like(gate)
    earlier = jnp.tril(jnp.ones((token_count, token_count), jnp.bool_), -1)
    same = (routing[:, None] == routing[None, :]) & earlier
    slots = routing * capacity + jnp.sum(same.astype(jnp.int32), axis=1)
    row = jnp.arange(columns * capacity, dtype=jnp.int32)
    device, place = row // capacity, row % capacity
    row_key = (device // groups_per * capacity + place) * 2 + device % 2
    column_key = jnp.concatenate([2 * slots, 2 * slots + 1])
    table = (row_key[:, None] == column_key[None, :]).astype(bf16)

    held = jnp.stack([pick(tokens), pick(out_grad)])
    sent = jnp.concatenate([held, came_rows], axis=2).astype(f32)
    sent = (jnp.stack([ones, gate]) * sent).astype(bf16).reshape(2 * token_count, wide)
    packed = jnp.dot(table, sent, preferred_element_type=f32).astype(bf16)
    packed = packed.reshape(columns, capacity, wide)
    rows = lax.all_to_all(packed, "expert", 0, 0, tiled=True)
    rows = rows.reshape(columns * capacity, wide)
    other_rows = lax.ppermute(rows, "expert", swap_core)

    parts = jnp.concatenate(
        [
            jnp.dot(one, weight, preferred_element_type=f32)
            .astype(bf16)
            .reshape(lines, -1, hidden_cols)
            for one, weight in ((rows, first), (other_rows, second))
        ],
        axis=1,
    )
    got = lax.all_to_all(parts, "dp", 0, 0, axis_index_groups=peers, tiled=True)
    total = jnp.sum(got.astype(f32), axis=0)
    left, right = total[: total.shape[0] // 2], total[total.shape[0] // 2 :]
    on_first = (lax.axis_index("expert") & 1) < 1
    pre, back = jnp.where(on_first, left, right), jnp.where(on_first, right, left)
    hidden, preact_grad = jax.nn.silu(pre), back * silu_grad(pre)
    share = jnp.concatenate(
        [
            jnp.where(on_first, hidden, preact_grad).astype(bf16),
            jnp.where(on_first, preact_grad, hidden).astype(bf16),
        ],
        axis=1,
    )
    share = jnp.broadcast_to(share[None], (lines,) + share.shape)
    full = lax.all_to_all(share, "dp", 0, 0, axis_index_groups=peers, tiled=True)
    full = full.reshape(-1, 2 * hidden_cols)
    kept, given = full[:, :hidden_cols], full[:, hidden_cols:]

    first, second = lax.optimization_barrier((first, second))
    part = lax.dot_general(given, first, contract_last, preferred_element_type=f32)
    came_part = lax.ppermute(part.astype(bf16), "expert", swap_core)
    part = lax.dot_general(kept, second, contract_last, preferred_element_type=f32)
    chip_sum = (part + came_part.astype(f32)).astype(bf16)
    home = lax.all_to_all(
        chip_sum.reshape(columns, capacity, wide), "expert", 0, 0, tiled=True
    )
    summed = lax.dot_general(
        table, home.reshape(-1, wide), contract_first, preferred_element_type=f32
    )
    done = (jnp.stack([gate, ones]) * summed.reshape(2, token_count, wide)).astype(bf16)
    came_done = lax.ppermute(done[:, :, features:], "dp", swap_side)
    own_done = done[:, :, :features]
    is_mine = (jnp.arange(micro_count) == 1)[:, None, None] == on_second

    def grad_of(rows_of, columns_of):
        whole = lax.dot_general(
            rows_of, columns_of, contract_first, preferred_element_type=f32
        )
        came = lax.ppermute(whole[features:].astype(bf16), "dp", swap_side)
        return (whole[:features] + came.astype(f32)).astype(bf16)

    grad_first = grad_of(rows, given)
    grad_second = grad_of(other_rows, kept)
    return (
        jnp.where(is_mine, own_done[0][None], came_done[0][None]),
        jnp.where(is_mine, own_done[1][None], came_done[1][None]),
        jnp.where(first_core, grad_first, grad_second),
        jnp.where(first_core, grad_second, grad_first).T,
    )


def solution(mesh):
    in_specs = (
        P(None, "expert", "dp"),
        P(None, "expert", "dp"),
        P(None, "expert", None),
        P(None, "expert", None),
        P("dp", "expert"),
        P("expert", "dp"),
    )
    out_specs = (
        P(None, "expert", "dp"),
        P(None, "expert", "dp"),
        P("dp", "expert"),
        P("expert", "dp"),
    )
    return jax.shard_map(
        on_device, mesh=mesh, in_specs=in_specs, out_specs=out_specs, check_vma=False
    )
```

```python
import jax
import jax.numpy as jnp
from jax import lax
from jax.sharding import PartitionSpec as P

FF = 2048


def silu_grad(preact):
    logistic = jax.nn.sigmoid(preact)
    return logistic * (1.0 + preact * (1.0 - logistic))


def on_device(tokens, out_grad, expert_ids, gate_weights, w_up, w_down):
    micro_count, token_count, features = tokens.shape
    hidden_cols = w_up.shape[1]
    columns = lax.axis_size("expert")
    dp = lax.axis_size("dp")
    lines = dp // 2
    groups_per = FF // hidden_cols
    chips_per = groups_per // 2
    experts = columns // groups_per
    capacity = 2 * token_count // experts
    wide = 2 * features
    bf16 = jnp.bfloat16
    f32 = jnp.float32
    contract_last = (((1,), (1,)), ((), ()))
    contract_first = (((0,), (0,)), ((), ()))
    swap_core = [(i, i ^ 1) for i in range(columns)]
    swap_side = [(i, i ^ 2) for i in range(dp)]
    peers = [[i for i in range(dp) if i // 2 % 2 == side] for side in range(2)]
    first_core = (lax.axis_index("expert") & 1) == 0
    on_second = (lax.axis_index("dp") & 2) == 2

    def pick(array):
        return jnp.where(on_second, array[1], array[0])

    given = jnp.stack(
        [jnp.where(on_second, array[0], array[1]) for array in (tokens, out_grad)]
    )
    came_rows = lax.ppermute(given, "dp", swap_side)

    w_down_t = w_down.T
    weights = jnp.concatenate(
        [jnp.where(first_core, w_up, w_down_t), jnp.where(first_core, w_down_t, w_up)], axis=1
    )
    weights = jnp.concatenate([weights, lax.ppermute(weights, "dp", swap_side)], axis=0)

    routing = pick(expert_ids)[:, 0]
    gate = pick(gate_weights)
    ones = jnp.ones_like(gate)
    earlier = jnp.tril(jnp.ones((token_count, token_count), jnp.bool_), -1)
    same = (routing[:, None] == routing[None, :]) & earlier
    slots = routing * capacity + jnp.sum(same.astype(jnp.int32), axis=1)
    row = jnp.arange(columns * capacity, dtype=jnp.int32)
    device, place = row // capacity, row % capacity
    row_key = (device // groups_per * capacity + place) * 2 + device % 2
    column_key = jnp.concatenate([2 * slots, 2 * slots + 1])
    table = (row_key[:, None] == column_key[None, :]).astype(bf16)

    held = jnp.stack([pick(tokens), pick(out_grad)])
    sent = jnp.concatenate([held, came_rows], axis=2).astype(f32)
    sent = (jnp.stack([ones, gate]) * sent).astype(bf16).reshape(2 * token_count, wide)
    packed = jnp.dot(table, sent, preferred_element_type=f32).astype(bf16)
    packed = packed.reshape(columns, capacity, wide)
    rows = lax.all_to_all(packed, "expert", 0, 0, tiled=True)
    rows = rows.reshape(columns * capacity, wide)
    rows, weights = lax.optimization_barrier((rows, weights))
    first, second = weights[:, :hidden_cols], weights[:, hidden_cols:]
    other_rows = lax.ppermute(rows, "expert", swap_core)

    parts = jnp.concatenate(
        [
            jnp.dot(one, weight, preferred_element_type=f32)
            .astype(bf16)
            .reshape(lines, -1, hidden_cols)
            for one, weight in ((rows, first), (other_rows, second))
        ],
        axis=1,
    )
    got = lax.all_to_all(parts, "dp", 0, 0, axis_index_groups=peers, tiled=True)
    total = jnp.sum(got.astype(f32), axis=0)
    left, right = total[: total.shape[0] // 2], total[total.shape[0] // 2 :]
    on_first = (lax.axis_index("expert") & 1) < 1
    pre, back = jnp.where(on_first, left, right), jnp.where(on_first, right, left)
    hidden, preact_grad = jax.nn.silu(pre), back * silu_grad(pre)
    share = jnp.concatenate(
        [
            jnp.where(on_first, hidden, preact_grad).astype(bf16),
            jnp.where(on_first, preact_grad, hidden).astype(bf16),
        ],
        axis=1,
    )
    share = jnp.broadcast_to(share[None], (lines,) + share.shape)
    full = lax.all_to_all(share, "dp", 0, 0, axis_index_groups=peers, tiled=True)
    full = full.reshape(-1, 2 * hidden_cols)
    kept, given = full[:, :hidden_cols], full[:, hidden_cols:]

    first, second = lax.optimization_barrier((first, second))
    part = lax.dot_general(given, first, contract_last, preferred_element_type=f32)
    came_part = lax.ppermute(part.astype(bf16), "expert", swap_core)
    part = lax.dot_general(kept, second, contract_last, preferred_element_type=f32)
    chip_sum = (part + came_part.astype(f32)).astype(bf16)
    home = lax.all_to_all(
        chip_sum.reshape(columns, capacity, wide), "expert", 0, 0, tiled=True
    )
    summed = lax.dot_general(
        table, home.reshape(-1, wide), contract_first, preferred_element_type=f32
    )
    done = (jnp.stack([gate, ones]) * summed.reshape(2, token_count, wide)).astype(bf16)

    wholes = [
        lax.dot_general(rows_of, columns_of, contract_first, preferred_element_type=f32)
        for rows_of, columns_of in ((rows, given), (other_rows, kept))
    ]
    came = [
        lax.ppermute(whole[features:].astype(bf16), "dp", swap_side) for whole in wholes
    ]
    came_done = lax.ppermute(done[:, :, features:], "dp", swap_side)
    came_done, came = lax.optimization_barrier((came_done, came))
    own_done = done[:, :, :features]
    is_mine = (jnp.arange(micro_count) == 1)[:, None, None] == on_second
    grad_first, grad_second = [
        (whole[:features] + part.astype(f32)).astype(bf16)
        for whole, part in zip(wholes, came)
    ]
    return (
        jnp.where(is_mine, own_done[0][None], came_done[0][None]),
        jnp.where(is_mine, own_done[1][None], came_done[1][None]),
        jnp.where(first_core, grad_first, grad_second),
        jnp.where(first_core, grad_second, grad_first).T,
    )


def solution(mesh):
    in_specs = (
        P(None, "expert", "dp"),
        P(None, "expert", "dp"),
        P(None, "expert", None),
        P(None, "expert", None),
        P("dp", "expert"),
        P("expert", "dp"),
    )
    out_specs = (
        P(None, "expert", "dp"),
        P(None, "expert", "dp"),
        P("dp", "expert"),
        P("expert", "dp"),
    )
    return jax.shard_map(
        on_device, mesh=mesh, in_specs=in_specs, out_specs=out_specs, check_vma=False
    )
```

```python
import jax
import jax.numpy as jnp
from jax import lax
from jax.sharding import PartitionSpec as P

FF = 2048


def silu_grad(preact):
    logistic = jax.nn.sigmoid(preact)
    return logistic * (1.0 + preact * (1.0 - logistic))


def on_device(tokens, out_grad, expert_ids, gate_weights, w_up, w_down):
    micro_count, token_count, features = tokens.shape
    hidden_cols = w_up.shape[1]
    columns = lax.axis_size("expert")
    dp = lax.axis_size("dp")
    lines = dp // 2
    groups_per = FF // hidden_cols
    chips_per = groups_per // 2
    experts = columns // groups_per
    capacity = 2 * token_count // experts
    wide = 2 * features
    bf16 = jnp.bfloat16
    f32 = jnp.float32
    contract_last = (((1,), (1,)), ((), ()))
    contract_first = (((0,), (0,)), ((), ()))
    swap_core = [(i, i ^ 1) for i in range(columns)]
    swap_side = [(i, i ^ 2) for i in range(dp)]
    peers = [[i for i in range(dp) if i // 2 % 2 == side] for side in range(2)]
    first_core = (lax.axis_index("expert") & 1) == 0
    on_second = (lax.axis_index("dp") & 2) == 2

    def pick(array):
        return jnp.where(on_second, array[1], array[0])

    given = jnp.stack(
        [jnp.where(on_second, array[0], array[1]) for array in (tokens, out_grad)]
    )
    came_rows = lax.ppermute(given, "dp", swap_side)

    w_down_t = w_down.T
    weights = jnp.concatenate(
        [jnp.where(first_core, w_up, w_down_t), jnp.where(first_core, w_down_t, w_up)], axis=1
    )
    weights = jnp.concatenate([weights, lax.ppermute(weights, "dp", swap_side)], axis=0)

    routing = pick(expert_ids)[:, 0]
    gate = pick(gate_weights)
    ones = jnp.ones_like(gate)
    earlier = jnp.tril(jnp.ones((token_count, token_count), jnp.bool_), -1)
    same = (routing[:, None] == routing[None, :]) & earlier
    slots = routing * capacity + jnp.sum(same.astype(jnp.int32), axis=1)
    row = jnp.arange(columns * capacity, dtype=jnp.int32)
    device, place = row // capacity, row % capacity
    row_key = (device // groups_per * capacity + place) * 2 + device % 2
    column_key = jnp.concatenate([2 * slots, 2 * slots + 1])
    table = (row_key[:, None] == column_key[None, :]).astype(bf16)

    held = jnp.stack([pick(tokens), pick(out_grad)])
    sent = jnp.concatenate([held, came_rows], axis=2).astype(f32)
    sent = (jnp.stack([ones, gate]) * sent).astype(bf16).reshape(2 * token_count, wide)
    packed = jnp.dot(table, sent, preferred_element_type=f32).astype(bf16)
    packed = packed.reshape(columns, capacity, wide)
    rows = lax.all_to_all(packed, "expert", 0, 0, tiled=True)
    rows = rows.reshape(columns * capacity, wide)
    rows, weights = lax.optimization_barrier((rows, weights))
    first, second = weights[:, :hidden_cols], weights[:, hidden_cols:]
    other_rows = lax.ppermute(rows, "expert", swap_core)

    parts = jnp.concatenate(
        [
            jnp.dot(one, weight, preferred_element_type=f32)
            .astype(bf16)
            .reshape(lines, -1, hidden_cols)
            for one, weight in ((rows, first), (other_rows, second))
        ],
        axis=1,
    )
    got = lax.all_to_all(parts, "dp", 0, 0, axis_index_groups=peers, tiled=True)
    total = jnp.sum(got.astype(f32), axis=0)
    left, right = total[: total.shape[0] // 2], total[total.shape[0] // 2 :]
    on_first = (lax.axis_index("expert") & 1) < 1
    pre, back = jnp.where(on_first, left, right), jnp.where(on_first, right, left)
    hidden, preact_grad = jax.nn.silu(pre), back * silu_grad(pre)
    share = jnp.concatenate(
        [
            jnp.where(on_first, hidden, preact_grad).astype(bf16),
            jnp.where(on_first, preact_grad, hidden).astype(bf16),
        ],
        axis=1,
    )
    share = jnp.broadcast_to(share[None], (lines,) + share.shape)
    full = lax.all_to_all(share, "dp", 0, 0, axis_index_groups=peers, tiled=True)
    full = full.reshape(-1, 2 * hidden_cols)
    kept, given = full[:, :hidden_cols], full[:, hidden_cols:]

    first, second = lax.optimization_barrier((first, second))
    part = lax.dot_general(given, first, contract_last, preferred_element_type=f32)
    came_part = lax.ppermute(part.astype(bf16), "expert", swap_core)
    part = lax.dot_general(kept, second, contract_last, preferred_element_type=f32)
    chip_sum = (part + came_part.astype(f32)).astype(bf16)
    home = lax.all_to_all(
        chip_sum.reshape(columns, capacity, wide), "expert", 0, 0, tiled=True
    )
    summed = lax.dot_general(
        table, home.reshape(-1, wide), contract_first, preferred_element_type=f32
    )
    done = (jnp.stack([gate, ones]) * summed.reshape(2, token_count, wide)).astype(bf16)

    wholes = [
        lax.dot_general(
            rows_of, columns_of, contract_first, preferred_element_type=f32
        ).astype(bf16)
        for rows_of, columns_of in ((rows, given), (other_rows, kept))
    ]
    came = [lax.ppermute(whole[features:], "dp", swap_side) for whole in wholes]
    came_done = lax.ppermute(done[:, :, features:], "dp", swap_side)
    done, came = lax.optimization_barrier((done, came))
    own_done = done[:, :, :features]
    is_mine = (jnp.arange(micro_count) == 1)[:, None, None] == on_second
    grad_first, grad_second = [
        (whole[:features].astype(f32) + part.astype(f32)).astype(bf16)
        for whole, part in zip(wholes, came)
    ]
    return (
        jnp.where(is_mine, own_done[0][None], came_done[0][None]),
        jnp.where(is_mine, own_done[1][None], came_done[1][None]),
        jnp.where(first_core, grad_first, grad_second),
        jnp.where(first_core, grad_second, grad_first).T,
    )


def solution(mesh):
    in_specs = (
        P(None, "expert", "dp"),
        P(None, "expert", "dp"),
        P(None, "expert", None),
        P(None, "expert", None),
        P("dp", "expert"),
        P("expert", "dp"),
    )
    out_specs = (
        P(None, "expert", "dp"),
        P(None, "expert", "dp"),
        P("dp", "expert"),
        P("expert", "dp"),
    )
    return jax.shard_map(
        on_device, mesh=mesh, in_specs=in_specs, out_specs=out_specs, check_vma=False
    )
```

```python
import jax
import jax.numpy as jnp
from jax import lax
from jax.sharding import PartitionSpec as P

FF = 2048


def silu_grad(preact):
    logistic = jax.nn.sigmoid(preact)
    return logistic * (1.0 + preact * (1.0 - logistic))


def on_device(tokens, out_grad, expert_ids, gate_weights, w_up, w_down):
    micro_count, token_count, features = tokens.shape
    hidden_cols = w_up.shape[1]
    columns = lax.axis_size("expert")
    dp = lax.axis_size("dp")
    lines = dp // 2
    groups_per = FF // hidden_cols
    chips_per = groups_per // 2
    experts = columns // groups_per
    capacity = 2 * token_count // experts
    wide = 2 * features
    bf16 = jnp.bfloat16
    f32 = jnp.float32
    contract_last = (((1,), (1,)), ((), ()))
    contract_first = (((0,), (0,)), ((), ()))
    swap_core = [(i, i ^ 1) for i in range(columns)]
    swap_side = [(i, i ^ 2) for i in range(dp)]
    peers = [[i for i in range(dp) if i // 2 % 2 == side] for side in range(2)]
    first_core = (lax.axis_index("expert") & 1) == 0
    on_second = (lax.axis_index("dp") & 2) == 2

    def pick(array):
        return jnp.where(on_second, array[1], array[0])

    given = jnp.stack(
        [jnp.where(on_second, array[0], array[1]) for array in (tokens, out_grad)]
    )
    came_rows = lax.ppermute(given, "dp", swap_side)

    w_down_t = w_down.T
    weights = jnp.concatenate(
        [jnp.where(first_core, w_up, w_down_t), jnp.where(first_core, w_down_t, w_up)], axis=1
    )
    weights = jnp.concatenate([weights, lax.ppermute(weights, "dp", swap_side)], axis=0)

    routing = pick(expert_ids)[:, 0]
    gate = pick(gate_weights)
    ones = jnp.ones_like(gate)
    earlier = jnp.tril(jnp.ones((token_count, token_count), jnp.bool_), -1)
    same = (routing[:, None] == routing[None, :]) & earlier
    slots = routing * capacity + jnp.sum(same.astype(jnp.int32), axis=1)
    row = jnp.arange(columns * capacity, dtype=jnp.int32)
    device, place = row // capacity, row % capacity
    row_key = (device // groups_per * capacity + place) * 2 + device % 2
    column_key = jnp.concatenate([2 * slots, 2 * slots + 1])
    table = (row_key[:, None] == column_key[None, :]).astype(bf16)

    held = jnp.stack([pick(tokens), pick(out_grad)])
    sent = jnp.concatenate([held, came_rows], axis=2).astype(f32)
    sent = (jnp.stack([ones, gate]) * sent).astype(bf16).reshape(2 * token_count, wide)
    packed = jnp.dot(table, sent, preferred_element_type=f32).astype(bf16)
    packed = packed.reshape(columns, capacity, wide)
    rows = lax.all_to_all(packed, "expert", 0, 0, tiled=True)
    rows = rows.reshape(columns * capacity, wide)
    rows, weights = lax.optimization_barrier((rows, weights))
    first, second = weights[:, :hidden_cols], weights[:, hidden_cols:]
    other_rows = lax.ppermute(rows, "expert", swap_core)

    parts = jnp.concatenate(
        [
            jnp.dot(one, weight, preferred_element_type=f32)
            .astype(bf16)
            .reshape(lines, -1, hidden_cols)
            for one, weight in ((rows, first), (other_rows, second))
        ],
        axis=1,
    )
    got = lax.all_to_all(parts, "dp", 0, 0, axis_index_groups=peers, tiled=True)
    total = jnp.sum(got.astype(f32), axis=0)
    left, right = total[: total.shape[0] // 2], total[total.shape[0] // 2 :]
    on_first = (lax.axis_index("expert") & 1) < 1
    pre, back = jnp.where(on_first, left, right), jnp.where(on_first, right, left)
    hidden, preact_grad = jax.nn.silu(pre), back * silu_grad(pre)
    share = jnp.concatenate(
        [
            jnp.where(on_first, hidden, preact_grad).astype(bf16),
            jnp.where(on_first, preact_grad, hidden).astype(bf16),
        ],
        axis=1,
    )
    share = jnp.broadcast_to(share[None], (lines,) + share.shape)
    full = lax.all_to_all(share, "dp", 0, 0, axis_index_groups=peers, tiled=True)
    full = full.reshape(-1, 2 * hidden_cols)
    kept, given = full[:, :hidden_cols], full[:, hidden_cols:]

    part = lax.dot_general(given, first, contract_last, preferred_element_type=f32)
    came_part = lax.ppermute(part.astype(bf16), "expert", swap_core)
    part = lax.dot_general(kept, second, contract_last, preferred_element_type=f32)
    chip_sum = (part + came_part.astype(f32)).astype(bf16)
    home = lax.all_to_all(
        chip_sum.reshape(columns, capacity, wide), "expert", 0, 0, tiled=True
    )
    summed = lax.dot_general(
        table, home.reshape(-1, wide), contract_first, preferred_element_type=f32
    )
    done = (jnp.stack([gate, ones]) * summed.reshape(2, token_count, wide)).astype(bf16)

    wholes = [
        lax.dot_general(
            rows_of, columns_of, contract_first, preferred_element_type=f32
        ).astype(bf16)
        for rows_of, columns_of in ((rows, given), (other_rows, kept))
    ]
    came = [lax.ppermute(whole[features:], "dp", swap_side) for whole in wholes]
    came_done = lax.ppermute(done[:, :, features:], "dp", swap_side)
    done, came = lax.optimization_barrier((done, came))
    own_done = done[:, :, :features]
    is_mine = (jnp.arange(micro_count) == 1)[:, None, None] == on_second
    grad_first, grad_second = [
        (whole[:features].astype(f32) + part.astype(f32)).astype(bf16)
        for whole, part in zip(wholes, came)
    ]
    return (
        jnp.where(is_mine, own_done[0][None], came_done[0][None]),
        jnp.where(is_mine, own_done[1][None], came_done[1][None]),
        jnp.where(first_core, grad_first, grad_second),
        jnp.where(first_core, grad_second, grad_first).T,
    )


def solution(mesh):
    in_specs = (
        P(None, "expert", "dp"),
        P(None, "expert", "dp"),
        P(None, "expert", None),
        P(None, "expert", None),
        P("dp", "expert"),
        P("expert", "dp"),
    )
    out_specs = (
        P(None, "expert", "dp"),
        P(None, "expert", "dp"),
        P("dp", "expert"),
        P("expert", "dp"),
    )
    return jax.shard_map(
        on_device, mesh=mesh, in_specs=in_specs, out_specs=out_specs, check_vma=False
    )
```

```python
import jax
import jax.numpy as jnp
from jax import lax
from jax.sharding import PartitionSpec as P

FF = 2048


def silu_grad(preact):
    logistic = jax.nn.sigmoid(preact)
    return logistic * (1.0 + preact * (1.0 - logistic))


def on_device(tokens, out_grad, expert_ids, gate_weights, w_up, w_down):
    micro_count, token_count, features = tokens.shape
    hidden_cols = w_up.shape[1]
    columns = lax.axis_size("expert")
    dp = lax.axis_size("dp")
    lines = dp // 2
    groups_per = FF // hidden_cols
    chips_per = groups_per // 2
    experts = columns // groups_per
    capacity = 2 * token_count // experts
    wide = 2 * features
    bf16 = jnp.bfloat16
    f32 = jnp.float32
    contract_last = (((1,), (1,)), ((), ()))
    contract_first = (((0,), (0,)), ((), ()))
    swap_core = [(i, i ^ 1) for i in range(columns)]
    swap_side = [(i, i ^ 2) for i in range(dp)]
    peers = [[i for i in range(dp) if i // 2 % 2 == side] for side in range(2)]
    first_core = (lax.axis_index("expert") & 1) == 0
    on_second = (lax.axis_index("dp") & 2) == 2

    def pick(array):
        return jnp.where(on_second, array[1], array[0])

    given = jnp.stack(
        [jnp.where(on_second, array[0], array[1]) for array in (tokens, out_grad)]
    )
    came_rows = lax.ppermute(given, "dp", swap_side)

    w_down_t = w_down.T
    weights = jnp.concatenate(
        [jnp.where(first_core, w_up, w_down_t), jnp.where(first_core, w_down_t, w_up)], axis=1
    )
    weights = jnp.concatenate([weights, lax.ppermute(weights, "dp", swap_side)], axis=0)

    routing = pick(expert_ids)[:, 0]
    gate = pick(gate_weights)
    ones = jnp.ones_like(gate)
    earlier = jnp.tril(jnp.ones((token_count, token_count), jnp.bool_), -1)
    same = (routing[:, None] == routing[None, :]) & earlier
    slots = routing * capacity + jnp.sum(same.astype(jnp.int32), axis=1)
    row = jnp.arange(columns * capacity, dtype=jnp.int32)
    device, place = row // capacity, row % capacity
    row_key = (device // groups_per * capacity + place) * 2 + device % 2
    column_key = jnp.concatenate([2 * slots, 2 * slots + 1])
    table = (row_key[:, None] == column_key[None, :]).astype(bf16)

    held = jnp.stack([pick(tokens), pick(out_grad)])
    sent = jnp.concatenate([held, came_rows], axis=2).astype(f32)
    sent = (jnp.stack([ones, gate]) * sent).astype(bf16).reshape(2 * token_count, wide)
    packed = jnp.dot(table, sent, preferred_element_type=f32).astype(bf16)
    packed = packed.reshape(columns, capacity, wide)
    rows = lax.all_to_all(packed, "expert", 0, 0, tiled=True)
    rows = rows.reshape(columns * capacity, wide)
    rows, weights = lax.optimization_barrier((rows, weights))
    first, second = weights[:, :hidden_cols], weights[:, hidden_cols:]
    other_rows = lax.ppermute(rows, "expert", swap_core)

    parts = jnp.concatenate(
        [
            jnp.dot(one, weight, preferred_element_type=f32)
            .astype(bf16)
            .reshape(lines, -1, hidden_cols)
            for one, weight in ((rows, first), (other_rows, second))
        ],
        axis=1,
    )
    got = lax.all_to_all(parts, "dp", 0, 0, axis_index_groups=peers, tiled=True)
    total = jnp.sum(got.astype(f32), axis=0)
    left, right = total[: total.shape[0] // 2], total[total.shape[0] // 2 :]
    pre, back = jnp.where(first_core, left, right), jnp.where(first_core, right, left)
    hidden, preact_grad = jax.nn.silu(pre), back * silu_grad(pre)
    share = jnp.concatenate(
        [
            jnp.where(first_core, hidden, preact_grad).astype(bf16),
            jnp.where(first_core, preact_grad, hidden).astype(bf16),
        ],
        axis=1,
    )
    share = jnp.broadcast_to(share[None], (lines,) + share.shape)
    full = lax.all_to_all(share, "dp", 0, 0, axis_index_groups=peers, tiled=True)
    full = full.reshape(-1, 2 * hidden_cols)
    kept, given = full[:, :hidden_cols], full[:, hidden_cols:]

    part = lax.dot_general(given, first, contract_last, preferred_element_type=f32)
    came_part = lax.ppermute(part.astype(bf16), "expert", swap_core)
    part = lax.dot_general(kept, second, contract_last, preferred_element_type=f32)
    chip_sum = (part + came_part.astype(f32)).astype(bf16)
    home = lax.all_to_all(
        chip_sum.reshape(columns, capacity, wide), "expert", 0, 0, tiled=True
    )
    summed = lax.dot_general(
        table, home.reshape(-1, wide), contract_first, preferred_element_type=f32
    )
    done = (jnp.stack([gate, ones]) * summed.reshape(2, token_count, wide)).astype(bf16)

    wholes = [
        lax.dot_general(
            rows_of, columns_of, contract_first, preferred_element_type=f32
        ).astype(bf16)
        for rows_of, columns_of in ((rows, given), (other_rows, kept))
    ]
    came = [lax.ppermute(whole[features:], "dp", swap_side) for whole in wholes]
    came_done = lax.ppermute(done[:, :, features:], "dp", swap_side)
    done, came = lax.optimization_barrier((done, came))
    own_done = done[:, :, :features]
    is_mine = (jnp.arange(micro_count) == 1)[:, None, None] == on_second
    grad_first, grad_second = [
        (whole[:features].astype(f32) + part.astype(f32)).astype(bf16)
        for whole, part in zip(wholes, came)
    ]
    return (
        jnp.where(is_mine, own_done[0][None], came_done[0][None]),
        jnp.where(is_mine, own_done[1][None], came_done[1][None]),
        jnp.where(first_core, grad_first, grad_second),
        jnp.where(first_core, grad_second, grad_first).T,
    )


def solution(mesh):
    in_specs = (
        P(None, "expert", "dp"),
        P(None, "expert", "dp"),
        P(None, "expert", None),
        P(None, "expert", None),
        P("dp", "expert"),
        P("expert", "dp"),
    )
    out_specs = (
        P(None, "expert", "dp"),
        P(None, "expert", "dp"),
        P("dp", "expert"),
        P("expert", "dp"),
    )
    return jax.shard_map(
        on_device, mesh=mesh, in_specs=in_specs, out_specs=out_specs, check_vma=False
    )
```
